32 devices in a mesh: groups: 2 (over x), tensor: 8 (over z, y), side: 2 (over core).
Axes of the slice: x: 2, y: 2, z: 4, core: 2. Of those that a mesh axis runs over, the one named last changes fastest.
Arguments:
- hidden_in: bfloat16 [96, 16384], P('groups', ('tensor', 'side')), parts along dimension 0, may hold values from -600 to 600
- norm_gain: float32 [16384], replicated, may hold values from 0.1 to 1.9
- w_query: bfloat16 [16384, 16384], P(None, ('tensor', 'side')), may hold values from -0.046875 to 0.046875
- key_projection: bfloat16 [16384, 1024], P(None, ('tensor', 'side')), may hold values from -0.046875 to 0.046875
- value_projection: bfloat16 [16384, 1024], P(None, ('tensor', 'side')), may hold values from -0.046875 to 0.046875
- w_out: bfloat16 [16384, 16384], P(None, ('tensor', 'side')), may hold values from -0.046875 to 0.046875
- paged_key_cache: bfloat16 [512, 64, 1024], P(('groups', 'tensor', 'side')), parts along dimension 0, may hold values from -4 to 4
- paged_value_cache: bfloat16 [512, 64, 1024], P(('groups', 'tensor', 'side')), parts along dimension 0, may hold values from -4 to 4
- key_scale: float32 [512, 8], P(('groups', 'tensor', 'side')), parts along dimension 0, may hold values from 0.5 to 200
- value_page_scale: float32 [512, 8], P(('groups', 'tensor', 'side')), parts along dimension 0, may hold values from 0.5 to 2
- row_owner: int32 [96, 1], P('groups'), parts along dimension 0, may hold values from 0 to 15; in each aligned block of 48 rows (0 to 47, 48 to 95, ...) at most 4 rows name the same one
- lengths: int32 [96], P('groups'), parts along dimension 0, may hold values from 1 to 256, 7680 in all
- page_table: int32 [32, 16], P(('groups', 'tensor', 'side')), parts along dimension 0, may hold values from 0 to 15, each once within a row
Outputs:
- attn_out: bfloat16 [96, 16384], P('groups', ('tensor', 'side')), parts along dimension 0
The draws below stay inside these ranges and needn't reach their ends.
There are 2 independent parts, one for each index of `groups`. The reference program is written for one: setup_inputs(seed, part) draws one part's arguments, and reference() takes and returns one part's arrays. A program takes and returns all parts, laid end to end along the dimension named above; an argument that names none is the same for every part. Nothing has to cross between parts.
Inputs may be any that keep to these rules, and one draw needn't show every extreme that they name: `row_owner`: at most 4 rows name one owner; some owner is named by exactly 4 rows and every owner by at least one. `lengths`: some row has exactly 256 cached tokens. Each row of page_table holds every number from 0 to 15 once.
All inputs are finite; a program needn't handle non-finite values.
Results may differ from the reference program's by a relative error of at most 0.006.
The reference program's roundings to bfloat16 on the way count: a program that leaves them out, or rounds other values in their place, can miss the bound.
Values may be sent and summed in bfloat16 or wider, within the bound.
A program may use at most 192 MiB of HBM per device.

```python
import math
import jax
import jax.numpy as jnp
import numpy as np
from jax import lax

MODEL_WIDTH = 16384
QUERY_HEADS = 128
KEY_VALUE_HEADS = 8
HEAD_SIZE = 128
PAGE_TOKENS = 64
SLOT_PAGES = 4
GROUP_OWNERS = 16
ROWS = 48
OWNER_ROW_SLOTS = 4
OWNER_PAGES = 16
MAX_ROW_TOKENS = 256


def draw_hidden_in(key, part):
    key = jax.random.fold_in(key, 11)
    key_base, key_rows, key_columns = jax.random.split(key, 3)
    base_values = jnp.clip(jax.random.normal(key_base, (ROWS, MODEL_WIDTH), jnp.float32), -4.0, 4.0)
    log_top = math.log(10.0)
    row_factor = jnp.exp(jax.random.uniform(key_rows, (ROWS, 1), jnp.float32, 0.0, log_top))
    col_factor = jnp.exp(jax.random.uniform(key_columns, (1, MODEL_WIDTH), jnp.float32, 0.0, log_top))
    return (base_values * row_factor * col_factor).astype(jnp.bfloat16)


def draw_key_scale(key, part):
    key = jax.random.fold_in(key, 23)
    key_base = jax.random.fold_in(key, 0)
    full_shape = (GROUP_OWNERS * OWNER_PAGES, KEY_VALUE_HEADS)
    scales = jnp.exp(jax.random.uniform(key_base, full_shape, jnp.float32, math.log(0.5), math.log(2.0)))
    return scales.astype(jnp.float32)


def levels(rng, extent, cuts, least, top_value):
    gain, own = 1.0, jax.random.fold_in(rng, 6)
    for position, shards_of in cuts:
        heights = jnp.exp(jax.random.uniform(jax.random.fold_in(own, position), (shards_of,), jnp.float32, least / len(cuts), top_value / len(cuts)))
        gain = gain * jnp.repeat(heights, extent[position] // shards_of).reshape([-1 if axis == position else 1 for axis in range(len(extent))])
    return gain


def split_up(amount, total, most, skew):
    weights = [(1 << 20) // math.isqrt(standing ** skew) + 1 for standing in range(2, amount + 1)]
    rest, counts = total - most - (amount - 1), [1] * (amount - 1)
    while rest > 0:
        free = [i for i in range(amount - 1) if counts[i] < most]
        pool, remaining = sum([weights[i] for i in free]), rest
        for i in free:
            addition = min(most - counts[i], max(1, remaining * weights[i] // pool), rest)
            counts[i] = counts[i] + addition
            rest = rest - addition
    return np.array([most] + counts)


def uneven(own_key, count, total, reach, skew):
    if count == 2:
        one = jax.random.randint(own_key, (), max(1, total - reach), min(reach, total - 1) + 1)
        return jnp.stack([one, total - one])
    tallies = jnp.asarray(split_up(count, total, reach, skew), jnp.int32)
    couples = (count - 1) // 2
    source_of, taker = tallies[1:1 + 2 * couples:2], tallies[2:2 + 2 * couples:2]
    margin = jnp.minimum(source_of - 1, reach - taker)
    passed = jax.random.randint(jax.random.fold_in(own_key, 1), (couples,), 0, 1 << 20) % (margin + 1)
    tallies = tallies.at[1:1 + 2 * couples:2].set(source_of - passed).at[2:2 + 2 * couples:2].set(taker + passed)
    return tallies[jax.random.permutation(jax.random.fold_in(own_key, 2), count)]


def assign_block(rng, own, number, rows, number_of, top, most, slope):
    order = jax.random.permutation(rng, number_of)
    heavy_load, usual = shares(number_of, rows * top, most, slope, True), shares(number_of, rows * top, most, slope, False)
    places = jnp.arange(number_of)

    def named(sizes, rotation):
        used = int((sizes > 0).sum())
        fixed = max(1, used // 4)
        shifted = fixed + (places - fixed + rotation * (used - fixed)) % max(1, number_of - fixed)
        return jnp.zeros((number_of,), jnp.int32).at[order[jnp.where(places < fixed, places, shifted)]].set(jnp.asarray(sizes, jnp.int32))

    sizes = jnp.where(number % 4 == 0, named(heavy_load, number // 4), named(usual, number - number // 4 - 1))
    mixed = jax.random.permutation(jax.random.fold_in(own, 3), number_of)
    source_of, taker = mixed[0:number_of // 2 * 2:2], mixed[1:number_of // 2 * 2:2]
    room = jnp.minimum(sizes[source_of] - 1, most - sizes[taker]) // 2
    room = jnp.where((source_of == order[0]) | (taker == order[0]) | (sizes[taker] == 0), 0, jnp.maximum(room, 0))
    shifted = jax.random.randint(jax.random.fold_in(own, 4), (number_of // 2,), 0, 1 << 20) % (room + 1)
    sizes = sizes.at[source_of].add(-shifted).at[taker].add(shifted)
    members = jnp.searchsorted(jnp.cumsum(sizes), jnp.arange(rows * top), side="right").astype(jnp.int32)
    grid = members.reshape(top, rows).T
    grid = grid[jax.random.permutation(jax.random.fold_in(own, 1), rows)]
    rotation = jax.random.randint(jax.random.fold_in(own, 2), (rows, 1), 0, top)
    return jnp.take_along_axis(grid, (jnp.arange(top)[None, :] + rotation) % top, axis=1)


def shares(count, total, limit, lean, full):
    weights = [(1 << 20) // math.isqrt(grade ** lean) + 1 for grade in range(1, count + 1)]
    largest = limit if full else min(limit, max(-(-total // count), total * weights[0] // sum(weights)))
    least = 1 if total - largest >= count - 1 else 0
    given, surplus = [largest] + [least] * (count - 1), total - largest - least * (count - 1)
    while surplus > 0:
        candidates = [i for i in range(1, count) if given[i] < largest] or [i for i in range(1, count) if given[i] < limit]
        whole, left = sum([weights[i] for i in candidates]), surplus
        for i in candidates:
            addition = min(limit - given[i], max(1, left * weights[i] // whole), surplus)
            given[i] = given[i] + addition
            surplus = surplus - addition
    return np.array(given)


def scatter_about(stream_key, dims, width, bound, cuts=(), held_as=jnp.bfloat16):
    factor_of = levels(stream_key, dims, cuts, -0.22, 0.18) if cuts else 1.0
    array = jax.random.normal(stream_key, dims, jnp.float32) * width * factor_of
    return jnp.minimum(jnp.maximum(array, -bound), bound).astype(held_as)


def setup_inputs(seed: int = 0, part: int = 0) -> dict:
    seeds = jax.random.split(jax.random.key(seed), 14)
    part_keys = jax.random.split(jax.random.fold_in(seeds[13], part), 14)
    hidden_in = draw_hidden_in(jax.random.fold_in(jax.random.fold_in(seeds[13], part), 71), part)
    norm_gain = jnp.clip(1.0 + 0.18 * jax.random.normal(seeds[1], (MODEL_WIDTH,), jnp.float32), 0.1, 1.9)
    w_query = scatter_about(seeds[2], (MODEL_WIDTH, QUERY_HEADS * HEAD_SIZE), MODEL_WIDTH ** -0.5, 0.046875, ((1, 16),))
    key_projection = scatter_about(seeds[3], (MODEL_WIDTH, KEY_VALUE_HEADS * HEAD_SIZE), MODEL_WIDTH ** -0.5, 0.046875, ((1, 16),))
    value_projection = scatter_about(seeds[4], (MODEL_WIDTH, KEY_VALUE_HEADS * HEAD_SIZE), MODEL_WIDTH ** -0.5, 0.046875, ((1, 16),))
    w_out = scatter_about(seeds[5], (QUERY_HEADS * HEAD_SIZE, MODEL_WIDTH), (QUERY_HEADS * HEAD_SIZE) ** -0.5, 0.046875, ((1, 16),))
    paged_key_cache = scatter_about(part_keys[6], (GROUP_OWNERS * OWNER_PAGES, PAGE_TOKENS, KEY_VALUE_HEADS * HEAD_SIZE), 1.0, 4.0, ((0, 16),))
    paged_value_cache = scatter_about(part_keys[7], (GROUP_OWNERS * OWNER_PAGES, PAGE_TOKENS, KEY_VALUE_HEADS * HEAD_SIZE), 1.0, 4.0, ((0, 16),))
    key_scale = draw_key_scale(jax.random.fold_in(jax.random.fold_in(seeds[13], part), 71), part)
    value_page_scale = jnp.clip(jnp.exp(math.log(2.0) - 1.3862944 * jax.random.uniform(part_keys[9], (GROUP_OWNERS * OWNER_PAGES, KEY_VALUE_HEADS), jnp.float32) ** levels(part_keys[9], (GROUP_OWNERS * OWNER_PAGES, KEY_VALUE_HEADS), ((0, 16),), -0.2, 0.2)), 0.5, 2.0)
    row_owner_keys = jax.random.split(jax.random.fold_in(part_keys[10], 1), ROWS // ROWS)
    row_owner_turns = jax.random.permutation(jax.random.fold_in(part_keys[10], 3), ROWS // ROWS)
    row_owner = jax.vmap(lambda own, number: assign_block(jax.random.fold_in(part_keys[10], 2), own, number, ROWS, GROUP_OWNERS, 1, OWNER_ROW_SLOTS, 1))(row_owner_keys, row_owner_turns).reshape((ROWS, 1))
    lengths = uneven(part_keys[11], ROWS, ROWS * MAX_ROW_TOKENS * 5 // 8, MAX_ROW_TOKENS, 1).astype(jnp.int32)
    page_table = jax.vmap(lambda own: jax.random.permutation(own, OWNER_PAGES))(jax.random.split(part_keys[12], GROUP_OWNERS)).reshape((GROUP_OWNERS, OWNER_PAGES)).astype(jnp.int32)
    return {"hidden_in": hidden_in, "norm_gain": norm_gain, "w_query": w_query, "key_projection": key_projection, "value_projection": value_projection, "w_out": w_out, "paged_key_cache": paged_key_cache, "paged_value_cache": paged_value_cache, "key_scale": key_scale, "value_page_scale": value_page_scale, "row_owner": row_owner, "lengths": lengths, "page_table": page_table}


def rotation_angles(vectors, token_position):
    half_size = vectors.shape[-1] // 2
    exponent = jnp.arange(half_size, dtype=jnp.float32) * (-2.0 / vectors.shape[-1])
    frequency = jnp.power(jnp.float32(500000.0), exponent)
    angles = token_position * frequency
    cosine = jnp.cos(angles)
    sine_part = jnp.sin(angles)
    first = vectors[..., :half_size]
    second = vectors[..., half_size:]
    return jnp.concatenate([first * cosine - second * sine_part, second * cosine + first * sine_part], axis=-1)

def reference(hidden_in, norm_gain, w_query, key_projection, value_projection, w_out, paged_key_cache, paged_value_cache, key_scale, value_page_scale, row_owner, lengths, page_table):
    widened = hidden_in.astype(jnp.float32)
    mean_square = lax.optimization_barrier(jnp.mean(widened * widened, axis=1, keepdims=True))
    normed = (widened * lax.rsqrt(mean_square + 1e-05) * norm_gain).astype(jnp.bfloat16)
    query = jnp.dot(normed, w_query, preferred_element_type=jnp.float32).astype(jnp.bfloat16)
    key_new = jnp.dot(normed, key_projection, preferred_element_type=jnp.float32).astype(jnp.bfloat16)
    value_new = jnp.dot(normed, value_projection, preferred_element_type=jnp.float32).astype(jnp.bfloat16)
    owner_ids = row_owner[:, 0]
    row_numbers = jnp.arange(owner_ids.shape[0])
    same_owner = owner_ids[:, None] == owner_ids[None, :]
    earlier = row_numbers[None, :] < row_numbers[:, None]
    slot_index = lax.optimization_barrier(jnp.sum(jnp.where(same_owner & earlier, 1, 0), axis=1)).astype(jnp.int32)
    query_group_count = QUERY_HEADS // KEY_VALUE_HEADS
    inv_root = 1.0 / math.sqrt(HEAD_SIZE)

    def one_row(packed):
        query_row, single_key_row, single_value_row, owner_id, slot_id, length = packed
        local_pages = lax.dynamic_slice_in_dim(page_table[owner_id], (slot_id * SLOT_PAGES).astype(jnp.int32), SLOT_PAGES)
        page_numbers = (owner_id * OWNER_PAGES + local_pages).astype(jnp.int32)
        stored_keys = paged_key_cache[page_numbers].reshape(MAX_ROW_TOKENS, KEY_VALUE_HEADS, HEAD_SIZE).astype(jnp.float32)
        stored_values = paged_value_cache[page_numbers].reshape(MAX_ROW_TOKENS, KEY_VALUE_HEADS, HEAD_SIZE).astype(jnp.float32)
        key_factor = jnp.repeat(key_scale[page_numbers], PAGE_TOKENS, axis=0).T * inv_root
        value_factor = jnp.repeat(value_page_scale[page_numbers], PAGE_TOKENS, axis=0).T
        token_position = length.astype(jnp.float32)
        quantized_query = rotation_angles(query_row.astype(jnp.float32).reshape(QUERY_HEADS, HEAD_SIZE), token_position).astype(jnp.bfloat16)
        quantized_query = lax.optimization_barrier(quantized_query)
        turned_query = quantized_query.astype(jnp.float32).reshape(KEY_VALUE_HEADS, query_group_count, HEAD_SIZE)
        quantized_key = rotation_angles(single_key_row.astype(jnp.float32).reshape(KEY_VALUE_HEADS, HEAD_SIZE), token_position).astype(jnp.bfloat16)
        quantized_key = lax.optimization_barrier(quantized_key)
        turned_key = quantized_key.astype(jnp.float32)
        scores = jnp.einsum('gjd,tgd->gjt', turned_query, stored_keys) * key_factor[:, None, :]
        own_score = jnp.einsum('gjd,gd->gj', turned_query, turned_key) * inv_root
        live = jnp.arange(MAX_ROW_TOKENS) < length
        masked = jnp.where(live, scores, -jnp.inf)
        highest = jnp.maximum(lax.optimization_barrier(jnp.max(masked, axis=-1)), own_score)
        exponents = jnp.where(live, jnp.exp(masked - highest[..., None]), 0.0)
        own_exp = jnp.exp(own_score - highest)
        denominator = lax.optimization_barrier(jnp.sum(exponents, axis=-1)) + own_exp
        weights = (exponents / denominator[..., None] * value_factor[:, None, :]).astype(jnp.bfloat16)
        local_weight_sum = (own_exp / denominator).astype(jnp.bfloat16)
        blended_output = jnp.einsum('gjt,tgd->gjd', weights.astype(jnp.float32), stored_values)
        blended_output = blended_output + local_weight_sum.astype(jnp.float32)[..., None] * single_value_row.astype(jnp.float32).reshape(KEY_VALUE_HEADS, HEAD_SIZE)[:, None, :]
        return blended_output.reshape(QUERY_HEADS * HEAD_SIZE).astype(jnp.bfloat16)
    attention = lax.map(one_row, (query, key_new, value_new, owner_ids, slot_index, lengths))
    return jnp.dot(attention, w_out, preferred_element_type=jnp.float32).astype(jnp.bfloat16)
```

```python
import functools
import math

import jax
import jax.numpy as jnp
from jax import lax
from jax.experimental import pallas as pl
from jax.experimental.pallas import tpu as pltpu
from jax.sharding import PartitionSpec as P

QUERY_HEADS = 128
KEY_VALUE_HEADS = 8
HEAD_SIZE = 128
PAGE_TOKENS = 64
SLOT_PAGES = 4
OWNER_ROW_SLOTS = 4
MAX_ROW_TOKENS = 256


def rotation_angles(vectors, token_position):
    half_size = vectors.shape[-1] // 2
    exponent = jnp.arange(half_size, dtype=jnp.float32) * (-2.0 / vectors.shape[-1])
    frequency = jnp.power(jnp.float32(500000.0), exponent)
    angles = token_position * frequency
    cosine = jnp.cos(angles)
    sine_part = jnp.sin(angles)
    first = vectors[..., :half_size]
    second = vectors[..., half_size:]
    return jnp.concatenate(
        [first * cosine - second * sine_part, second * cosine + first * sine_part], axis=-1
    )

MESH = pl.DeviceIdType.MESH
GROUP_QUERIES = QUERY_HEADS // KEY_VALUE_HEADS
GROUP_WIDTH = GROUP_QUERIES * HEAD_SIZE
INV_ROOT = 1.0 / math.sqrt(HEAD_SIZE)


def place():
    tensor = lax.axis_index("tensor")
    return tensor // 2, lax.rem(tensor, 2), lax.axis_index("side"), lax.axis_size("tensor") // 2


def line_order(z, count):
    sign = 1 - 2 * (z // (count // 2))
    return [lax.rem(z + sign * k + count, count) for k in range(count)]


def enter():
    z, y, s, count = place()
    barrier = pltpu.get_barrier_semaphore()
    peers = [(zz * 2 + y, s) for zz in line_order(z, count)[1:]]
    peers += [(z * 2 + 1 - y, s), (z * 2 + y, 1 - s)]
    for tensor, side in peers:
        pl.semaphore_signal(
            barrier, inc=1, device_id={"tensor": tensor, "side": side}, device_id_type=MESH
        )
    pl.semaphore_wait(barrier, len(peers))


def gather(buffer, send_sems, recv_sems):
    z, y, s, count = place()
    line = line_order(z, count)
    started = []

    def index(zz, yy, ss):
        return (zz * 2 + yy) * 2 + ss

    def send(block, tensor, side):
        copy = pltpu.make_async_remote_copy(
            src_ref=buffer.at[block],
            dst_ref=buffer.at[block],
            send_sem=send_sems.at[len(started)],
            recv_sem=recv_sems.at[block],
            device_id={"tensor": tensor, "side": side},
            device_id_type=MESH,
        )
        copy.start()
        started.append(copy)

    def arrived(block):
        pltpu.make_async_remote_copy(
            src_ref=buffer.at[block],
            dst_ref=buffer.at[block],
            send_sem=send_sems.at[0],
            recv_sem=recv_sems.at[block],
            device_id={"tensor": z * 2 + y, "side": 1 - s},
            device_id_type=MESH,
        ).wait_recv()

    me = index(z, y, s)
    for zz in line[1:]:
        send(me, zz * 2 + y, s)
    send(me, z * 2 + 1 - y, s)
    send(me, z * 2 + y, 1 - s)
    for k in range(1, count + 1):
        if k < count:
            block = index(line[k], y, s)
            arrived(block)
            send(block, z * 2 + 1 - y, s)
            send(block, z * 2 + y, 1 - s)
        block = index(line[k - 1], 1 - y, s)
        arrived(block)
        send(block, z * 2 + y, 1 - s)
    for zz in line:
        for yy in (y, 1 - y):
            arrived(index(zz, yy, 1 - s))
    return started


def project_kernel(
    owners, x_ref, gain_ref, wq_hbm, key_hbm, value_hbm, out_ref,
    buffer, wq_ref, kv_ref, total, total_kv, w_sems, kv_sems, send_sems, recv_sems,
):
    depth = x_ref.shape[1]
    kv_columns = key_hbm.shape[0]
    query_columns = wq_hbm.shape[1]

    def weights(c):
        rows = pl.ds(pl.multiple_of(c * depth, depth), depth)
        return pltpu.make_async_copy(wq_hbm.at[rows, :], wq_ref.at[rows, :], w_sems.at[c])

    key_copy = pltpu.make_async_copy(key_hbm, kv_ref.at[0], kv_sems.at[0])
    value_copy = pltpu.make_async_copy(value_hbm, kv_ref.at[1], kv_sems.at[1])
    key_copy.start()
    value_copy.start()

    @pl.loop(0, owners)
    def _(c):
        weights(c).start()

    z, y, s, _ = place()
    buffer[(z * 2 + y) * 2 + s] = x_ref[...]
    enter()
    started = gather(buffer, send_sems, recv_sems)

    def squares(c, acc):
        x = buffer[c].astype(jnp.float32)
        return acc + jnp.sum(x * x, axis=1, keepdims=True)

    sums = lax.fori_loop(0, owners, squares, jnp.zeros((x_ref.shape[0], 1), jnp.float32))
    scale = lax.rsqrt(sums * (1.0 / (owners * depth)) + 1e-05)
    total[...] = jnp.zeros_like(total)
    total_kv[...] = jnp.zeros_like(total_kv)
    key_copy.wait()
    value_copy.wait()

    @pl.loop(0, owners)
    def _(c):
        columns = pl.ds(pl.multiple_of(c * depth, depth), depth)
        x = buffer[c].astype(jnp.float32)
        normed = (x * scale * gain_ref[pl.ds(c, 1), :]).astype(jnp.bfloat16)
        both = kv_ref[:, :, columns]
        if kv_columns % 16 == 0:
            both = both.reshape(2 * kv_columns, depth)
            total_kv[...] += lax.dot_general(
                normed, both, (((1,), (1,)), ((), ())), preferred_element_type=jnp.float32
            )
        else:
            for half in range(2):
                total_kv[:, half * kv_columns : (half + 1) * kv_columns] += lax.dot_general(
                    normed, both[half], (((1,), (1,)), ((), ())),
                    preferred_element_type=jnp.float32,
                )
        weights(c).wait()
        total[...] += jnp.dot(normed, wq_ref[columns, :], preferred_element_type=jnp.float32)

    out_ref[:, :query_columns] = total[...].astype(jnp.bfloat16)
    out_ref[:, query_columns:] = total_kv[...].astype(jnp.bfloat16)
    for copy in started:
        copy.wait_send()


def project(owners, hidden_in, norm_gain, w_query, key_projection, value_projection):
    rows, depth = hidden_in.shape
    columns, kv_columns = w_query.shape[1], key_projection.shape[1]
    sends = owners - 1
    vmem, anywhere = pl.BlockSpec(memory_space=pltpu.VMEM), pl.BlockSpec(memory_space=pl.ANY)
    return pl.pallas_call(
        functools.partial(project_kernel, owners),
        out_shape=jax.ShapeDtypeStruct((rows, columns + 2 * kv_columns), jnp.bfloat16),
        in_specs=[vmem, vmem, anywhere, anywhere, anywhere],
        out_specs=vmem,
        scratch_shapes=[
            pltpu.VMEM((owners, rows, depth), jnp.bfloat16),
            pltpu.VMEM(w_query.shape, jnp.bfloat16),
            pltpu.VMEM((2, kv_columns, owners * depth), jnp.bfloat16),
            pltpu.VMEM((rows, columns), jnp.float32),
            pltpu.VMEM((rows, 2 * kv_columns), jnp.float32),
            pltpu.SemaphoreType.DMA((owners,)),
            pltpu.SemaphoreType.DMA((2,)),
            pltpu.SemaphoreType.DMA((sends,)),
            pltpu.SemaphoreType.DMA((owners,)),
        ],
        compiler_params=pltpu.CompilerParams(
            collective_id=0, has_side_effects=True, vmem_limit_bytes=46 * 2**20
        ),
    )(hidden_in, norm_gain.reshape(owners, depth), w_query, key_projection.T, value_projection.T)


def attend_kernel(
    owners, wo_hbm, keys_ref, values_ref, query_ref, key_ref, value_ref, key_factor_ref,
    value_factor_ref, live_ref, destination_ref, out_ref,
    wo_ref, mixed, buffer, picked, total, w_sems, send_sems, recv_sems,
):
    rows = out_ref.shape[0]
    tokens = keys_ref.shape[0]
    slot_queries = OWNER_ROW_SLOTS * GROUP_QUERIES

    def weights(g):
        part = pl.ds(pl.multiple_of(g * GROUP_WIDTH, GROUP_WIDTH), GROUP_WIDTH)
        return pltpu.make_async_copy(wo_hbm.at[part, :], wo_ref.at[part, :], w_sems.at[g])

    @pl.loop(0, KEY_VALUE_HEADS)
    def _(g):
        weights(g).start()

    def spread(block):
        wide = jnp.broadcast_to(
            block[:, None, :], (OWNER_ROW_SLOTS, GROUP_QUERIES, block.shape[-1])
        )
        return wide.reshape(slot_queries, block.shape[-1])

    live = spread(live_ref[...]) > 0.5
    for g in range(KEY_VALUE_HEADS):
        columns = slice(g * HEAD_SIZE, (g + 1) * HEAD_SIZE)
        query = query_ref[g]
        scores = lax.dot_general(
            query, keys_ref[:, columns], (((1,), (1,)), ((), ())),
            preferred_element_type=jnp.float32,
        ) * key_factor_ref[g : g + 1, :]
        own = jnp.sum(
            query.astype(jnp.float32) * spread(key_ref[:, columns]), axis=1, keepdims=True
        ) * INV_ROOT
        masked = jnp.where(live, scores, -jnp.inf)
        highest = jnp.maximum(jnp.max(masked, axis=1, keepdims=True), own)
        exponents = jnp.exp(masked - highest)
        own_exp = jnp.exp(own - highest)
        inverse = 1.0 / (jnp.sum(exponents, axis=1, keepdims=True) + own_exp)
        probability = (exponents * inverse * value_factor_ref[g : g + 1, :]).astype(jnp.bfloat16)
        own_weight = (own_exp * inverse).astype(jnp.bfloat16).astype(jnp.float32)
        mixed[g * slot_queries : (g + 1) * slot_queries, :] = jnp.dot(
            probability, values_ref[:, columns], preferred_element_type=jnp.float32
        ) + own_weight * spread(value_ref[:, columns])

    z, y, s, _ = place()
    me = (z * 2 + y) * 2 + s
    block_rows = KEY_VALUE_HEADS * OWNER_ROW_SLOTS
    for j in range(GROUP_QUERIES):
        buffer[me, :, j * HEAD_SIZE : (j + 1) * HEAD_SIZE] = mixed[
            pl.ds(j, block_rows, stride=GROUP_QUERIES), :
        ].astype(jnp.bfloat16)
    enter()
    started = gather(buffer, send_sems, recv_sems)

    per = min(owners, 16)
    step = KEY_VALUE_HEADS if owners <= 16 else 1
    lane = lax.broadcasted_iota(jnp.int32, (rows, per * block_rows), 1)
    slot = (lane >> 5) * OWNER_ROW_SLOTS + (lane & 3)
    head = (lane >> 2) & 7

    def pick_block(block):
        everything = buffer[pl.ds(block * per, per)].reshape(per * block_rows, GROUP_WIDTH)
        wanted = destination_ref[...] - block * (per * OWNER_ROW_SLOTS)
        chosen = jnp.where(slot == wanted, head, -1)
        for first in range(0, KEY_VALUE_HEADS, step):
            pick = jnp.concatenate(
                [
                    jnp.where(chosen == first + g, 1.0, 0.0).astype(jnp.bfloat16)
                    for g in range(step)
                ],
                axis=0,
            )
            found = (
                jnp.dot(pick, everything, preferred_element_type=jnp.float32)
                .astype(jnp.bfloat16)
                .reshape(step, rows, GROUP_WIDTH)
            )
            if per == owners:
                picked[first : first + step] = found
            else:
                picked[first : first + step] += found

    if per == owners:
        pick_block(0)
    else:
        picked[...] = jnp.zeros_like(picked)
        pl.loop(0, owners // per)(pick_block)
    total[...] = jnp.zeros_like(total)

    @pl.loop(0, KEY_VALUE_HEADS)
    def _(g):
        weights(g).wait()
        part = pl.ds(pl.multiple_of(g * GROUP_WIDTH, GROUP_WIDTH), GROUP_WIDTH)
        total[...] += jnp.dot(picked[g], wo_ref[part, :], preferred_element_type=jnp.float32)

    out_ref[...] = total[...].astype(jnp.bfloat16)
    for copy in started:
        copy.wait_send()


def attend(owners, rows, w_out, *operands):
    sends = owners - 1
    block_rows = KEY_VALUE_HEADS * OWNER_ROW_SLOTS
    vmem, anywhere = pl.BlockSpec(memory_space=pltpu.VMEM), pl.BlockSpec(memory_space=pl.ANY)
    return pl.pallas_call(
        functools.partial(attend_kernel, owners),
        out_shape=jax.ShapeDtypeStruct((rows, w_out.shape[1]), jnp.bfloat16),
        in_specs=[anywhere] + [vmem] * len(operands),
        out_specs=vmem,
        scratch_shapes=[
            pltpu.VMEM(w_out.shape, jnp.bfloat16),
            pltpu.VMEM((block_rows * GROUP_QUERIES, HEAD_SIZE), jnp.float32),
            pltpu.VMEM((owners, block_rows, GROUP_WIDTH), jnp.bfloat16),
            pltpu.VMEM((KEY_VALUE_HEADS, rows, GROUP_WIDTH), jnp.bfloat16),
            pltpu.VMEM((rows, w_out.shape[1]), jnp.float32),
            pltpu.SemaphoreType.DMA((KEY_VALUE_HEADS,)),
            pltpu.SemaphoreType.DMA((sends,)),
            pltpu.SemaphoreType.DMA((owners,)),
        ],
        compiler_params=pltpu.CompilerParams(
            collective_id=1, has_side_effects=True, vmem_limit_bytes=56 * 2**20
        ),
    )(w_out, *operands)


def per_device(
    hidden_in,
    norm_gain,
    w_query,
    key_projection,
    value_projection,
    w_out,
    paged_key_cache,
    paged_value_cache,
    key_scale,
    value_page_scale,
    row_owner,
    lengths,
    page_table,
):
    owners = lax.axis_size(("tensor", "side"))
    my_index = lax.axis_index(("tensor", "side"))
    row_count = hidden_in.shape[0]
    query_group_count = QUERY_HEADS // KEY_VALUE_HEADS
    packed = project(owners, hidden_in, norm_gain, w_query, key_projection, value_projection)
    owner_ids = row_owner[:, 0]
    row_numbers = jnp.arange(row_count)
    same_owner = owner_ids[:, None] == owner_ids[None, :]
    earlier = row_numbers[None, :] < row_numbers[:, None]
    slot_index = jnp.sum(jnp.where(same_owner & earlier, 1, 0), axis=1).astype(jnp.int32)
    destination = owner_ids * OWNER_ROW_SLOTS + slot_index
    feature_count = packed.shape[1]
    one_hot = (jnp.arange(owners * OWNER_ROW_SLOTS)[:, None] == destination[None, :]).astype(
        jnp.bfloat16
    )
    outgoing = jnp.dot(one_hot, packed, preferred_element_type=jnp.float32).astype(jnp.bfloat16)
    received_part = lax.all_to_all(
        outgoing.reshape(owners, OWNER_ROW_SLOTS, 1, feature_count),
        ("tensor", "side"),
        split_axis=0,
        concat_axis=2,
        tiled=True,
    )
    received_part = received_part.reshape(OWNER_ROW_SLOTS, owners, feature_count)
    query_columns = w_query.shape[1]
    key_columns = key_projection.shape[1]
    query_all = received_part[:, :, :query_columns].reshape(
        OWNER_ROW_SLOTS, QUERY_HEADS * HEAD_SIZE
    )
    every_key = received_part[:, :, query_columns : query_columns + key_columns].reshape(
        OWNER_ROW_SLOTS, KEY_VALUE_HEADS * HEAD_SIZE
    )
    every_value = received_part[:, :, query_columns + key_columns :].reshape(
        OWNER_ROW_SLOTS, KEY_VALUE_HEADS * HEAD_SIZE
    )
    mine = owner_ids == my_index
    slot_match = (jnp.arange(OWNER_ROW_SLOTS)[:, None] == slot_index[None, :]) & mine[None, :]
    slot_length = jnp.sum(jnp.where(slot_match, lengths[None, :], 0), axis=1)
    pages = page_table.shape[1]
    page_slot = jnp.arange(pages)
    holds = page_table[0][:, None] == jnp.arange(pages)[None, :]
    page_place = jnp.sum(jnp.where(holds, page_slot[:, None], 0), axis=0)
    token_in_row = (
        (page_place % SLOT_PAGES)[:, None] * PAGE_TOKENS + jnp.arange(PAGE_TOKENS)[None, :]
    ).reshape(1, pages * PAGE_TOKENS)
    token_slot = jnp.repeat(page_place // SLOT_PAGES, PAGE_TOKENS)[None, :]
    live = (
        (token_slot == jnp.arange(OWNER_ROW_SLOTS)[:, None])
        & (token_in_row < slot_length[:, None])
    ).astype(jnp.float32)
    key_factor = jnp.repeat(key_scale.T, PAGE_TOKENS, axis=1) * INV_ROOT
    value_factor = jnp.repeat(value_page_scale.T, PAGE_TOKENS, axis=1)
    token_position = slot_length.astype(jnp.float32)[:, None, None]
    turned_query = rotation_angles(
        query_all.astype(jnp.float32).reshape(OWNER_ROW_SLOTS, QUERY_HEADS, HEAD_SIZE),
        token_position,
    ).astype(jnp.bfloat16)
    turned_query = jnp.transpose(
        turned_query.reshape(
            OWNER_ROW_SLOTS, KEY_VALUE_HEADS, query_group_count, HEAD_SIZE
        ),
        (1, 0, 2, 3),
    ).reshape(KEY_VALUE_HEADS, OWNER_ROW_SLOTS * query_group_count, HEAD_SIZE)
    turned_key = (
        rotation_angles(
            every_key.astype(jnp.float32).reshape(OWNER_ROW_SLOTS, KEY_VALUE_HEADS, HEAD_SIZE),
            token_position,
        )
        .astype(jnp.bfloat16)
        .astype(jnp.float32)
        .reshape(OWNER_ROW_SLOTS, KEY_VALUE_HEADS * HEAD_SIZE)
    )
    return attend(
        owners,
        row_count,
        w_out,
        paged_key_cache.reshape(pages * PAGE_TOKENS, KEY_VALUE_HEADS * HEAD_SIZE),
        paged_value_cache.reshape(pages * PAGE_TOKENS, KEY_VALUE_HEADS * HEAD_SIZE),
        turned_query,
        turned_key,
        every_value.astype(jnp.float32),
        key_factor,
        value_factor,
        live,
        destination.astype(jnp.int32)[:, None],
    )


def solution(mesh):
    return jax.shard_map(
        per_device,
        mesh=mesh,
        in_specs=(
            P("groups", ("tensor", "side")),
            P(),
            P(None, ("tensor", "side")),
            P(None, ("tensor", "side")),
            P(None, ("tensor", "side")),
            P(None, ("tensor", "side")),
            P(("groups", "tensor", "side"), None, None),
            P(("groups", "tensor", "side"), None, None),
            P(("groups", "tensor", "side"), None),
            P(("groups", "tensor", "side"), None),
            P("groups", None),
            P("groups"),
            P(("groups", "tensor", "side"), None),
        ),
        out_specs=P("groups", ("tensor", "side")),
        check_vma=False,
    )
```

```python
import functools
import math

import jax
import jax.numpy as jnp
from jax import lax
from jax.experimental import pallas as pl
from jax.experimental.pallas import tpu as pltpu
from jax.sharding import PartitionSpec as P

QUERY_HEADS = 128
KEY_VALUE_HEADS = 8
HEAD_SIZE = 128
PAGE_TOKENS = 64
SLOT_PAGES = 4
OWNER_ROW_SLOTS = 4
MAX_ROW_TOKENS = 256


def rotation_angles(vectors, token_position):
    half_size = vectors.shape[-1] // 2
    exponent = jnp.arange(half_size, dtype=jnp.float32) * (-2.0 / vectors.shape[-1])
    frequency = jnp.power(jnp.float32(500000.0), exponent)
    angles = token_position * frequency
    cosine = jnp.cos(angles)
    sine_part = jnp.sin(angles)
    first = vectors[..., :half_size]
    second = vectors[..., half_size:]
    return jnp.concatenate(
        [first * cosine - second * sine_part, second * cosine + first * sine_part], axis=-1
    )

MESH = pl.DeviceIdType.MESH
GROUP_QUERIES = QUERY_HEADS // KEY_VALUE_HEADS
GROUP_WIDTH = GROUP_QUERIES * HEAD_SIZE
INV_ROOT = 1.0 / math.sqrt(HEAD_SIZE)


def place():
    tensor = lax.axis_index("tensor")
    return tensor // 2, lax.rem(tensor, 2), lax.axis_index("side"), lax.axis_size("tensor") // 2


def line_order(z, count):
    sign = 1 - 2 * (z // (count // 2))
    return [lax.rem(z + sign * k + count, count) for k in range(count)]


def enter():
    z, y, s, count = place()
    barrier = pltpu.get_barrier_semaphore()
    peers = [(zz * 2 + y, s) for zz in line_order(z, count)[1:]]
    peers += [(z * 2 + 1 - y, s), (z * 2 + y, 1 - s)]
    for tensor, side in peers:
        pl.semaphore_signal(
            barrier, inc=1, device_id={"tensor": tensor, "side": side}, device_id_type=MESH
        )
    pl.semaphore_wait(barrier, len(peers))


def gather(buffer, send_sems, recv_sems, pieces):
    z, y, s, count = place()
    size = buffer.shape[1] // pieces
    left = []

    def index(zz, yy, ss):
        return (zz * 2 + yy) * 2 + ss

    def when(have, action):
        if have is None:
            action()
        else:
            pl.when(have)(action)

    def copy(block, piece, tensor, side, slot):
        part = buffer.at[block, pl.ds(piece * size, size)]
        return pltpu.make_async_remote_copy(
            src_ref=part,
            dst_ref=part,
            send_sem=send_sems.at[slot],
            recv_sem=recv_sems.at[block, piece],
            device_id={"tensor": tensor, "side": side},
            device_id_type=MESH,
        )

    def send(have, block, piece, tensor, side):
        slot = len(left)
        when(have, lambda: copy(block, piece, tensor, side, slot).start())
        left.append(
            lambda: when(have, lambda: copy(block, piece, tensor, side, slot).wait_send())
        )

    def arrived(have, block, piece):
        when(have, lambda: copy(block, piece, z * 2 + y, 1 - s, 0).wait_recv())

    here, across = z * 2 + y, z * 2 + 1 - y
    me = index(z, y, s)
    for piece in range(pieces):
        send(z < count - 1, me, piece, here + 2, s)
        send(z > 0, me, piece, here - 2, s)
        send(None, me, piece, across, s)
        send(None, me, piece, here, 1 - s)
    for k in range(1, count + 1):
        for piece in range(pieces):
            if k < count:
                low, high = index(z - k, y, s), index(z + k, y, s)
                arrived(z >= k, low, piece)
                send((z >= k) & (z < count - 1), low, piece, here + 2, s)
                send(z >= k, low, piece, across, s)
                arrived(z + k < count, high, piece)
                send((z + k < count) & (z > 0), high, piece, here - 2, s)
                send(z + k < count, high, piece, across, s)
                send(z >= k, low, piece, here, 1 - s)
                send(z + k < count, high, piece, here, 1 - s)
            if k == 1:
                block = index(z, 1 - y, s)
                arrived(None, block, piece)
                send(None, block, piece, here, 1 - s)
            else:
                low, high = index(z - k + 1, 1 - y, s), index(z + k - 1, 1 - y, s)
                arrived(z >= k - 1, low, piece)
                send(z >= k - 1, low, piece, here, 1 - s)
                arrived(z + k - 1 < count, high, piece)
                send(z + k - 1 < count, high, piece, here, 1 - s)
    for zz in line_order(z, count):
        for yy in (y, 1 - y):
            for piece in range(pieces):
                arrived(None, index(zz, yy, 1 - s), piece)
    return left


def project_kernel(
    owners, pieces, x_ref, gain_ref, wq_hbm, key_hbm, value_hbm, out_ref,
    buffer, wq_ref, kv_ref, total, total_kv, w_sems, kv_sems, send_sems, recv_sems,
):
    depth = x_ref.shape[1]
    kv_columns = key_hbm.shape[0]
    query_columns = wq_hbm.shape[1]

    def weights(c):
        rows = pl.ds(pl.multiple_of(c * depth, depth), depth)
        return pltpu.make_async_copy(wq_hbm.at[rows, :], wq_ref.at[rows, :], w_sems.at[c])

    key_copy = pltpu.make_async_copy(key_hbm, kv_ref.at[0], kv_sems.at[0])
    value_copy = pltpu.make_async_copy(value_hbm, kv_ref.at[1], kv_sems.at[1])
    key_copy.start()
    value_copy.start()

    @pl.loop(0, owners)
    def _(c):
        weights(c).start()

    z, y, s, _ = place()
    buffer[(z * 2 + y) * 2 + s] = x_ref[...]
    enter()
    started = gather(buffer, send_sems, recv_sems, pieces)

    def squares(c, acc):
        x = buffer[c].astype(jnp.float32)
        return acc + jnp.sum(x * x, axis=1, keepdims=True)

    sums = lax.fori_loop(0, owners, squares, jnp.zeros((x_ref.shape[0], 1), jnp.float32))
    scale = lax.rsqrt(sums * (1.0 / (owners * depth)) + 1e-05)
    total[...] = jnp.zeros_like(total)
    total_kv[...] = jnp.zeros_like(total_kv)
    key_copy.wait()
    value_copy.wait()

    @pl.loop(0, owners)
    def _(c):
        columns = pl.ds(pl.multiple_of(c * depth, depth), depth)
        x = buffer[c].astype(jnp.float32)
        normed = (x * scale * gain_ref[pl.ds(c, 1), :]).astype(jnp.bfloat16)
        both = kv_ref[:, :, columns]
        if kv_columns % 16 == 0:
            both = both.reshape(2 * kv_columns, depth)
            total_kv[...] += lax.dot_general(
                normed, both, (((1,), (1,)), ((), ())), preferred_element_type=jnp.float32
            )
        else:
            for half in range(2):
                total_kv[:, half * kv_columns : (half + 1) * kv_columns] += lax.dot_general(
                    normed, both[half], (((1,), (1,)), ((), ())),
                    preferred_element_type=jnp.float32,
                )
        weights(c).wait()
        total[...] += jnp.dot(normed, wq_ref[columns, :], preferred_element_type=jnp.float32)

    out_ref[:, :query_columns] = total[...].astype(jnp.bfloat16)
    out_ref[:, query_columns:] = total_kv[...].astype(jnp.bfloat16)
    for wait in started:
        wait()


def project(owners, hidden_in, norm_gain, w_query, key_projection, value_projection):
    rows, depth = hidden_in.shape
    columns, kv_columns = w_query.shape[1], key_projection.shape[1]
    pieces = 3 if owners <= 16 else 1
    sends = (2 * owners - 3) * pieces
    vmem, anywhere = pl.BlockSpec(memory_space=pltpu.VMEM), pl.BlockSpec(memory_space=pl.ANY)
    return pl.pallas_call(
        functools.partial(project_kernel, owners, pieces),
        out_shape=jax.ShapeDtypeStruct((rows, columns + 2 * kv_columns), jnp.bfloat16),
        in_specs=[vmem, vmem, anywhere, anywhere, anywhere],
        out_specs=vmem,
        scratch_shapes=[
            pltpu.VMEM((owners, rows, depth), jnp.bfloat16),
            pltpu.VMEM(w_query.shape, jnp.bfloat16),
            pltpu.VMEM((2, kv_columns, owners * depth), jnp.bfloat16),
            pltpu.VMEM((rows, columns), jnp.float32),
            pltpu.VMEM((rows, 2 * kv_columns), jnp.float32),
            pltpu.SemaphoreType.DMA((owners,)),
            pltpu.SemaphoreType.DMA((2,)),
            pltpu.SemaphoreType.DMA((sends,)),
            pltpu.SemaphoreType.DMA((owners, pieces)),
        ],
        compiler_params=pltpu.CompilerParams(
            collective_id=0, has_side_effects=True, vmem_limit_bytes=58 * 2**20
        ),
    )(hidden_in, norm_gain.reshape(owners, depth), w_query, key_projection.T, value_projection.T)


def attend_kernel(
    owners, pieces, wo_hbm, keys_ref, values_ref, query_ref, key_ref, value_ref, key_factor_ref,
    value_factor_ref, live_ref, destination_ref, out_ref,
    wo_ref, mixed, buffer, picked, total, w_sems, send_sems, recv_sems,
):
    rows = out_ref.shape[0]
    tokens = keys_ref.shape[0]
    slot_queries = OWNER_ROW_SLOTS * GROUP_QUERIES

    def weights(g):
        part = pl.ds(pl.multiple_of(g * GROUP_WIDTH, GROUP_WIDTH), GROUP_WIDTH)
        return pltpu.make_async_copy(wo_hbm.at[part, :], wo_ref.at[part, :], w_sems.at[g])

    @pl.loop(0, KEY_VALUE_HEADS)
    def _(g):
        weights(g).start()

    def spread(block):
        wide = jnp.broadcast_to(
            block[:, None, :], (OWNER_ROW_SLOTS, GROUP_QUERIES, block.shape[-1])
        )
        return wide.reshape(slot_queries, block.shape[-1])

    live = spread(live_ref[...]) > 0.5
    for g in range(KEY_VALUE_HEADS):
        columns = slice(g * HEAD_SIZE, (g + 1) * HEAD_SIZE)
        query = query_ref[g]
        scores = lax.dot_general(
            query, keys_ref[:, columns], (((1,), (1,)), ((), ())),
            preferred_element_type=jnp.float32,
        ) * key_factor_ref[g : g + 1, :]
        own = jnp.sum(
            query.astype(jnp.float32) * spread(key_ref[:, columns]), axis=1, keepdims=True
        ) * INV_ROOT
        masked = jnp.where(live, scores, -jnp.inf)
        highest = jnp.maximum(jnp.max(masked, axis=1, keepdims=True), own)
        exponents = jnp.exp(masked - highest)
        own_exp = jnp.exp(own - highest)
        inverse = 1.0 / (jnp.sum(exponents, axis=1, keepdims=True) + own_exp)
        probability = (exponents * inverse * value_factor_ref[g : g + 1, :]).astype(jnp.bfloat16)
        own_weight = (own_exp * inverse).astype(jnp.bfloat16).astype(jnp.float32)
        mixed[g * slot_queries : (g + 1) * slot_queries, :] = jnp.dot(
            probability, values_ref[:, columns], preferred_element_type=jnp.float32
        ) + own_weight * spread(value_ref[:, columns])

    z, y, s, _ = place()
    me = (z * 2 + y) * 2 + s
    block_rows = KEY_VALUE_HEADS * OWNER_ROW_SLOTS
    for j in range(GROUP_QUERIES):
        buffer[me, :, j * HEAD_SIZE : (j + 1) * HEAD_SIZE] = mixed[
            pl.ds(j, block_rows, stride=GROUP_QUERIES), :
        ].astype(jnp.bfloat16)
    enter()
    started = gather(buffer, send_sems, recv_sems, pieces)

    per = min(owners, 16)
    step = KEY_VALUE_HEADS if owners <= 16 else 1
    lane = lax.broadcasted_iota(jnp.int32, (rows, per * block_rows), 1)
    slot = (lane >> 5) * OWNER_ROW_SLOTS + (lane & 3)
    head = (lane >> 2) & 7

    def pick_block(block):
        everything = buffer[pl.ds(block * per, per)].reshape(per * block_rows, GROUP_WIDTH)
        wanted = destination_ref[...] - block * (per * OWNER_ROW_SLOTS)
        chosen = jnp.where(slot == wanted, head, -1)
        for first in range(0, KEY_VALUE_HEADS, step):
            pick = jnp.concatenate(
                [
                    jnp.where(chosen == first + g, 1.0, 0.0).astype(jnp.bfloat16)
                    for g in range(step)
                ],
                axis=0,
            )
            found = (
                jnp.dot(pick, everything, preferred_element_type=jnp.float32)
                .astype(jnp.bfloat16)
                .reshape(step, rows, GROUP_WIDTH)
            )
            if per == owners:
                picked[first : first + step] = found
            else:
                picked[first : first + step] += found

    if per == owners:
        pick_block(0)
    else:
        picked[...] = jnp.zeros_like(picked)
        pl.loop(0, owners // per)(pick_block)
    total[...] = jnp.zeros_like(total)

    @pl.loop(0, KEY_VALUE_HEADS)
    def _(g):
        weights(g).wait()
        part = pl.ds(pl.multiple_of(g * GROUP_WIDTH, GROUP_WIDTH), GROUP_WIDTH)
        total[...] += jnp.dot(picked[g], wo_ref[part, :], preferred_element_type=jnp.float32)

    out_ref[...] = total[...].astype(jnp.bfloat16)
    for wait in started:
        wait()


def attend(owners, rows, w_out, *operands):
    pieces = 2 if owners <= 16 else 1
    sends = (2 * owners - 3) * pieces
    block_rows = KEY_VALUE_HEADS * OWNER_ROW_SLOTS
    vmem, anywhere = pl.BlockSpec(memory_space=pltpu.VMEM), pl.BlockSpec(memory_space=pl.ANY)
    return pl.pallas_call(
        functools.partial(attend_kernel, owners, pieces),
        out_shape=jax.ShapeDtypeStruct((rows, w_out.shape[1]), jnp.bfloat16),
        in_specs=[anywhere] + [vmem] * len(operands),
        out_specs=vmem,
        scratch_shapes=[
            pltpu.VMEM(w_out.shape, jnp.bfloat16),
            pltpu.VMEM((block_rows * GROUP_QUERIES, HEAD_SIZE), jnp.float32),
            pltpu.VMEM((owners, block_rows, GROUP_WIDTH), jnp.bfloat16),
            pltpu.VMEM((KEY_VALUE_HEADS, rows, GROUP_WIDTH), jnp.bfloat16),
            pltpu.VMEM((rows, w_out.shape[1]), jnp.float32),
            pltpu.SemaphoreType.DMA((KEY_VALUE_HEADS,)),
            pltpu.SemaphoreType.DMA((sends,)),
            pltpu.SemaphoreType.DMA((owners, pieces)),
        ],
        compiler_params=pltpu.CompilerParams(
            collective_id=1, has_side_effects=True, vmem_limit_bytes=56 * 2**20
        ),
    )(w_out, *operands)


def per_device(
    hidden_in,
    norm_gain,
    w_query,
    key_projection,
    value_projection,
    w_out,
    paged_key_cache,
    paged_value_cache,
    key_scale,
    value_page_scale,
    row_owner,
    lengths,
    page_table,
):
    owners = lax.axis_size(("tensor", "side"))
    my_index = lax.axis_index(("tensor", "side"))
    row_count = hidden_in.shape[0]
    query_group_count = QUERY_HEADS // KEY_VALUE_HEADS
    packed = project(owners, hidden_in, norm_gain, w_query, key_projection, value_projection)
    owner_ids = row_owner[:, 0]
    row_numbers = jnp.arange(row_count)
    same_owner = owner_ids[:, None] == owner_ids[None, :]
    earlier = row_numbers[None, :] < row_numbers[:, None]
    slot_index = jnp.sum(jnp.where(same_owner & earlier, 1, 0), axis=1).astype(jnp.int32)
    destination = owner_ids * OWNER_ROW_SLOTS + slot_index
    feature_count = packed.shape[1]
    one_hot = (jnp.arange(owners * OWNER_ROW_SLOTS)[:, None] == destination[None, :]).astype(
        jnp.bfloat16
    )
    outgoing = jnp.dot(one_hot, packed, preferred_element_type=jnp.float32).astype(jnp.bfloat16)
    received_part = lax.all_to_all(
        outgoing.reshape(owners, OWNER_ROW_SLOTS, 1, feature_count),
        ("tensor", "side"),
        split_axis=0,
        concat_axis=2,
        tiled=True,
    )
    received_part = received_part.reshape(OWNER_ROW_SLOTS, owners, feature_count)
    query_columns = w_query.shape[1]
    key_columns = key_projection.shape[1]
    query_all = received_part[:, :, :query_columns].reshape(
        OWNER_ROW_SLOTS, QUERY_HEADS * HEAD_SIZE
    )
    every_key = received_part[:, :, query_columns : query_columns + key_columns].reshape(
        OWNER_ROW_SLOTS, KEY_VALUE_HEADS * HEAD_SIZE
    )
    every_value = received_part[:, :, query_columns + key_columns :].reshape(
        OWNER_ROW_SLOTS, KEY_VALUE_HEADS * HEAD_SIZE
    )
    mine = owner_ids == my_index
    slot_match = (jnp.arange(OWNER_ROW_SLOTS)[:, None] == slot_index[None, :]) & mine[None, :]
    slot_length = jnp.sum(jnp.where(slot_match, lengths[None, :], 0), axis=1)
    pages = page_table.shape[1]
    page_slot = jnp.arange(pages)
    holds = page_table[0][:, None] == jnp.arange(pages)[None, :]
    page_place = jnp.sum(jnp.where(holds, page_slot[:, None], 0), axis=0)
    token_in_row = (
        (page_place % SLOT_PAGES)[:, None] * PAGE_TOKENS + jnp.arange(PAGE_TOKENS)[None, :]
    ).reshape(1, pages * PAGE_TOKENS)
    token_slot = jnp.repeat(page_place // SLOT_PAGES, PAGE_TOKENS)[None, :]
    live = (
        (token_slot == jnp.arange(OWNER_ROW_SLOTS)[:, None])
        & (token_in_row < slot_length[:, None])
    ).astype(jnp.float32)
    key_factor = jnp.repeat(key_scale.T, PAGE_TOKENS, axis=1) * INV_ROOT
    value_factor = jnp.repeat(value_page_scale.T, PAGE_TOKENS, axis=1)
    token_position = slot_length.astype(jnp.float32)[:, None, None]
    turned_query = rotation_angles(
        query_all.astype(jnp.float32).reshape(OWNER_ROW_SLOTS, QUERY_HEADS, HEAD_SIZE),
        token_position,
    ).astype(jnp.bfloat16)
    turned_query = jnp.transpose(
        turned_query.reshape(
            OWNER_ROW_SLOTS, KEY_VALUE_HEADS, query_group_count, HEAD_SIZE
        ),
        (1, 0, 2, 3),
    ).reshape(KEY_VALUE_HEADS, OWNER_ROW_SLOTS * query_group_count, HEAD_SIZE)
    turned_key = (
        rotation_angles(
            every_key.astype(jnp.float32).reshape(OWNER_ROW_SLOTS, KEY_VALUE_HEADS, HEAD_SIZE),
            token_position,
        )
        .astype(jnp.bfloat16)
        .astype(jnp.float32)
        .reshape(OWNER_ROW_SLOTS, KEY_VALUE_HEADS * HEAD_SIZE)
    )
    return attend(
        owners,
        row_count,
        w_out,
        paged_key_cache.reshape(pages * PAGE_TOKENS, KEY_VALUE_HEADS * HEAD_SIZE),
        paged_value_cache.reshape(pages * PAGE_TOKENS, KEY_VALUE_HEADS * HEAD_SIZE),
        turned_query,
        turned_key,
        every_value.astype(jnp.float32),
        key_factor,
        value_factor,
        live,
        destination.astype(jnp.int32)[:, None],
    )


def solution(mesh):
    return jax.shard_map(
        per_device,
        mesh=mesh,
        in_specs=(
            P("groups", ("tensor", "side")),
            P(),
            P(None, ("tensor", "side")),
            P(None, ("tensor", "side")),
            P(None, ("tensor", "side")),
            P(None, ("tensor", "side")),
            P(("groups", "tensor", "side"), None, None),
            P(("groups", "tensor", "side"), None, None),
            P(("groups", "tensor", "side"), None),
            P(("groups", "tensor", "side"), None),
            P("groups", None),
            P("groups"),
            P(("groups", "tensor", "side"), None),
        ),
        out_specs=P("groups", ("tensor", "side")),
        check_vma=False,
    )
```

```python
import functools
import math

import jax
import jax.numpy as jnp
from jax import lax
from jax.experimental import pallas as pl
from jax.experimental.pallas import tpu as pltpu
from jax.sharding import PartitionSpec as P

QUERY_HEADS = 128
KEY_VALUE_HEADS = 8
HEAD_SIZE = 128
PAGE_TOKENS = 64
SLOT_PAGES = 4
OWNER_ROW_SLOTS = 4
MAX_ROW_TOKENS = 256


def rotation_angles(vectors, token_position):
    half_size = vectors.shape[-1] // 2
    exponent = jnp.arange(half_size, dtype=jnp.float32) * (-2.0 / vectors.shape[-1])
    frequency = jnp.power(jnp.float32(500000.0), exponent)
    angles = token_position * frequency
    cosine = jnp.cos(angles)
    sine_part = jnp.sin(angles)
    first = vectors[..., :half_size]
    second = vectors[..., half_size:]
    return jnp.concatenate(
        [first * cosine - second * sine_part, second * cosine + first * sine_part], axis=-1
    )

MESH = pl.DeviceIdType.MESH
GROUP_QUERIES = QUERY_HEADS // KEY_VALUE_HEADS
GROUP_WIDTH = GROUP_QUERIES * HEAD_SIZE
INV_ROOT = 1.0 / math.sqrt(HEAD_SIZE)


def place():
    tensor = lax.axis_index("tensor")
    return tensor // 2, lax.rem(tensor, 2), lax.axis_index("side"), lax.axis_size("tensor") // 2


def line_order(z, count):
    sign = 1 - 2 * (z // (count // 2))
    return [lax.rem(z + sign * k + count, count) for k in range(count)]


def enter():
    z, y, s, count = place()
    barrier = pltpu.get_barrier_semaphore()
    peers = [(zz * 2 + y, s) for zz in line_order(z, count)[1:]]
    peers += [(z * 2 + 1 - y, s), (z * 2 + y, 1 - s)]
    for tensor, side in peers:
        pl.semaphore_signal(
            barrier, inc=1, device_id={"tensor": tensor, "side": side}, device_id_type=MESH
        )
    pl.semaphore_wait(barrier, len(peers))


def enter_all(owners):
    z, y, s, _ = place()
    me = (z * 2 + y) * 2 + s
    barrier = pltpu.get_barrier_semaphore()

    @pl.loop(1, owners)
    def _(k):
        other = lax.rem(me + k, owners)
        pl.semaphore_signal(
            barrier,
            inc=1,
            device_id={"tensor": other // 2, "side": lax.rem(other, 2)},
            device_id_type=MESH,
        )

    pl.semaphore_wait(barrier, owners - 1)


def gather(buffer, send_sems, recv_sems, pieces):
    z, y, s, count = place()
    size = buffer.shape[1] // pieces
    left = []

    def index(zz, yy, ss):
        return (zz * 2 + yy) * 2 + ss

    def when(have, action):
        if have is None:
            action()
        else:
            pl.when(have)(action)

    def copy(block, piece, tensor, side, slot):
        part = buffer.at[block, pl.ds(piece * size, size)]
        return pltpu.make_async_remote_copy(
            src_ref=part,
            dst_ref=part,
            send_sem=send_sems.at[slot],
            recv_sem=recv_sems.at[block, piece],
            device_id={"tensor": tensor, "side": side},
            device_id_type=MESH,
        )

    def send(have, block, piece, tensor, side):
        slot = len(left)
        when(have, lambda: copy(block, piece, tensor, side, slot).start())
        left.append(
            lambda: when(have, lambda: copy(block, piece, tensor, side, slot).wait_send())
        )

    def arrived(have, block, piece):
        when(have, lambda: copy(block, piece, z * 2 + y, 1 - s, 0).wait_recv())

    here, across = z * 2 + y, z * 2 + 1 - y
    me = index(z, y, s)
    for piece in range(pieces):
        send(z < count - 1, me, piece, here + 2, s)
        send(z > 0, me, piece, here - 2, s)
        send(None, me, piece, across, s)
        send(None, me, piece, here, 1 - s)
    for k in range(1, count + 1):
        for piece in range(pieces):
            if k < count:
                low, high = index(z - k, y, s), index(z + k, y, s)
                arrived(z >= k, low, piece)
                send((z >= k) & (z < count - 1), low, piece, here + 2, s)
                send(z >= k, low, piece, across, s)
                arrived(z + k < count, high, piece)
                send((z + k < count) & (z > 0), high, piece, here - 2, s)
                send(z + k < count, high, piece, across, s)
                send(z >= k, low, piece, here, 1 - s)
                send(z + k < count, high, piece, here, 1 - s)
            if k == 1:
                block = index(z, 1 - y, s)
                arrived(None, block, piece)
                send(None, block, piece, here, 1 - s)
            else:
                low, high = index(z - k + 1, 1 - y, s), index(z + k - 1, 1 - y, s)
                arrived(z >= k - 1, low, piece)
                send(z >= k - 1, low, piece, here, 1 - s)
                arrived(z + k - 1 < count, high, piece)
                send(z + k - 1 < count, high, piece, here, 1 - s)
    for zz in line_order(z, count):
        for yy in (y, 1 - y):
            for piece in range(pieces):
                arrived(None, index(zz, yy, 1 - s), piece)
    return left


def project_kernel(
    owners, pieces, x_ref, gain_ref, code_ref, wq_hbm, key_hbm, value_hbm, out_ref,
    buffer, wq_ref, kv_ref, total, total_kv, outbox, inbox,
    w_sems, kv_sems, send_sems, recv_sems, out_sems, in_sems,
):
    depth = x_ref.shape[1]
    kv_columns = key_hbm.shape[0]
    query_columns = wq_hbm.shape[1]

    def weights(c):
        rows = pl.ds(pl.multiple_of(c * depth, depth), depth)
        return pltpu.make_async_copy(wq_hbm.at[rows, :], wq_ref.at[rows, :], w_sems.at[c])

    key_copy = pltpu.make_async_copy(key_hbm, kv_ref.at[0], kv_sems.at[0])
    value_copy = pltpu.make_async_copy(value_hbm, kv_ref.at[1], kv_sems.at[1])
    key_copy.start()
    value_copy.start()

    @pl.loop(0, owners)
    def _(c):
        weights(c).start()

    z, y, s, _ = place()
    me = (z * 2 + y) * 2 + s
    buffer[me] = x_ref[...]
    enter_all(owners)
    started = gather(buffer, send_sems, recv_sems, pieces)

    def squares(c, acc):
        x = buffer[c].astype(jnp.float32)
        return acc + jnp.sum(x * x, axis=1, keepdims=True)

    sums = lax.fori_loop(0, owners, squares, jnp.zeros((x_ref.shape[0], 1), jnp.float32))
    scale = lax.rsqrt(sums * (1.0 / (owners * depth)) + 1e-05)
    total[...] = jnp.zeros_like(total)
    total_kv[...] = jnp.zeros_like(total_kv)
    key_copy.wait()
    value_copy.wait()

    @pl.loop(0, owners)
    def _(c):
        columns = pl.ds(pl.multiple_of(c * depth, depth), depth)
        x = buffer[c].astype(jnp.float32)
        normed = (x * scale * gain_ref[pl.ds(c, 1), :]).astype(jnp.bfloat16)
        both = kv_ref[:, :, columns]
        if kv_columns % 16 == 0:
            both = both.reshape(2 * kv_columns, depth)
            total_kv[...] += lax.dot_general(
                normed, both, (((1,), (1,)), ((), ())), preferred_element_type=jnp.float32
            )
        else:
            for half in range(2):
                total_kv[:, half * kv_columns : (half + 1) * kv_columns] += lax.dot_general(
                    normed, both[half], (((1,), (1,)), ((), ())),
                    preferred_element_type=jnp.float32,
                )
        weights(c).wait()
        total[...] += jnp.dot(normed, wq_ref[columns, :], preferred_element_type=jnp.float32)

    heads = query_columns // HEAD_SIZE
    slots = owners * OWNER_ROW_SLOTS
    shape = (owners, outbox.shape[1], code_ref.shape[1])
    inner = lax.broadcasted_iota(jnp.int32, shape, 1)
    wanted = (
        jnp.minimum(inner >> 2, heads) * slots
        + lax.broadcasted_iota(jnp.int32, shape, 0) * OWNER_ROW_SLOTS
        + (inner & 3)
    ).reshape(shape[0] * shape[1], shape[2])
    pick = jnp.where(wanted == code_ref[...], 1.0, 0.0).astype(jnp.bfloat16)
    both = total_kv[...].astype(jnp.bfloat16)
    if 2 * kv_columns < HEAD_SIZE:
        spare = jnp.zeros((both.shape[0], HEAD_SIZE - 2 * kv_columns), jnp.bfloat16)
        both = jnp.concatenate([both, spare], axis=1)
    stacked = [
        total[:, h * HEAD_SIZE : (h + 1) * HEAD_SIZE].astype(jnp.bfloat16) for h in range(heads)
    ]
    outbox[...] = (
        jnp.dot(
            pick,
            jnp.concatenate(stacked + [both], axis=0),
            preferred_element_type=jnp.float32,
        )
        .astype(jnp.bfloat16)
        .reshape(outbox.shape)
    )

    def delivery(k):
        other = lax.rem(me + k, owners)
        return pltpu.make_async_remote_copy(
            src_ref=outbox.at[other],
            dst_ref=inbox.at[me],
            send_sem=out_sems.at[other],
            recv_sem=in_sems.at[me],
            device_id={"tensor": other // 2, "side": lax.rem(other, 2)},
            device_id_type=MESH,
        )

    def receipt(k):
        other = lax.rem(me + k, owners)
        return pltpu.make_async_remote_copy(
            src_ref=outbox.at[other],
            dst_ref=inbox.at[other],
            send_sem=out_sems.at[other],
            recv_sem=in_sems.at[other],
            device_id={"tensor": other // 2, "side": lax.rem(other, 2)},
            device_id_type=MESH,
        )

    @pl.loop(1, owners)
    def _(k):
        delivery(k).start()

    inbox[me] = outbox[me]

    @pl.loop(1, owners)
    def _(k):
        receipt(k).wait_recv()

    out_ref[...] = inbox[...]

    @pl.loop(1, owners)
    def _(k):
        delivery(k).wait_send()

    for wait in started:
        wait()


def project(
    owners, destination, hidden_in, norm_gain, w_query, key_projection, value_projection
):
    rows, depth = hidden_in.shape
    columns, kv_columns = w_query.shape[1], key_projection.shape[1]
    heads = columns // HEAD_SIZE
    box = (owners, -(-(heads + 1) * OWNER_ROW_SLOTS // 16) * 16, HEAD_SIZE)
    code = (
        jnp.arange(heads + 1, dtype=jnp.int32)[:, None] * (owners * OWNER_ROW_SLOTS)
        + destination[None, :].astype(jnp.int32)
    ).reshape(1, (heads + 1) * rows)
    pieces = 3 if owners <= 16 else 1
    sends = (2 * owners - 3) * pieces
    vmem, anywhere = pl.BlockSpec(memory_space=pltpu.VMEM), pl.BlockSpec(memory_space=pl.ANY)
    return pl.pallas_call(
        functools.partial(project_kernel, owners, pieces),
        out_shape=jax.ShapeDtypeStruct(box, jnp.bfloat16),
        in_specs=[vmem, vmem, vmem, anywhere, anywhere, anywhere],
        out_specs=vmem,
        scratch_shapes=[
            pltpu.VMEM((owners, rows, depth), jnp.bfloat16),
            pltpu.VMEM(w_query.shape, jnp.bfloat16),
            pltpu.VMEM((2, kv_columns, owners * depth), jnp.bfloat16),
            pltpu.VMEM((rows, columns), jnp.float32),
            pltpu.VMEM((rows, 2 * kv_columns), jnp.float32),
            pltpu.VMEM(box, jnp.bfloat16),
            pltpu.VMEM(box, jnp.bfloat16),
            pltpu.SemaphoreType.DMA((owners,)),
            pltpu.SemaphoreType.DMA((2,)),
            pltpu.SemaphoreType.DMA((sends,)),
            pltpu.SemaphoreType.DMA((owners, pieces)),
            pltpu.SemaphoreType.DMA((owners,)),
            pltpu.SemaphoreType.DMA((owners,)),
        ],
        compiler_params=pltpu.CompilerParams(
            collective_id=0, has_side_effects=True, vmem_limit_bytes=58 * 2**20
        ),
    )(
        hidden_in,
        norm_gain.reshape(owners, depth),
        code,
        w_query,
        key_projection.T,
        value_projection.T,
    )


def attend_kernel(
    owners, pieces, wo_hbm, keys_ref, values_ref, query_ref, key_ref, value_ref, key_factor_ref,
    value_factor_ref, live_ref, destination_ref, out_ref,
    wo_ref, mixed, buffer, picked, total, w_sems, send_sems, recv_sems,
):
    rows = out_ref.shape[0]
    tokens = keys_ref.shape[0]
    slot_queries = OWNER_ROW_SLOTS * GROUP_QUERIES

    def weights(g):
        part = pl.ds(pl.multiple_of(g * GROUP_WIDTH, GROUP_WIDTH), GROUP_WIDTH)
        return pltpu.make_async_copy(wo_hbm.at[part, :], wo_ref.at[part, :], w_sems.at[g])

    @pl.loop(0, KEY_VALUE_HEADS)
    def _(g):
        weights(g).start()

    def spread(block):
        wide = jnp.broadcast_to(
            block[:, None, :], (OWNER_ROW_SLOTS, GROUP_QUERIES, block.shape[-1])
        )
        return wide.reshape(slot_queries, block.shape[-1])

    live = spread(live_ref[...]) > 0.5
    for g in range(KEY_VALUE_HEADS):
        columns = slice(g * HEAD_SIZE, (g + 1) * HEAD_SIZE)
        query = query_ref[g]
        scores = lax.dot_general(
            query, keys_ref[:, columns], (((1,), (1,)), ((), ())),
            preferred_element_type=jnp.float32,
        ) * key_factor_ref[g : g + 1, :]
        own = jnp.sum(
            query.astype(jnp.float32) * spread(key_ref[:, columns]), axis=1, keepdims=True
        ) * INV_ROOT
        masked = jnp.where(live, scores, -jnp.inf)
        highest = jnp.maximum(jnp.max(masked, axis=1, keepdims=True), own)
        exponents = jnp.exp(masked - highest)
        own_exp = jnp.exp(own - highest)
        inverse = 1.0 / (jnp.sum(exponents, axis=1, keepdims=True) + own_exp)
        probability = (exponents * inverse * value_factor_ref[g : g + 1, :]).astype(jnp.bfloat16)
        own_weight = (own_exp * inverse).astype(jnp.bfloat16).astype(jnp.float32)
        mixed[g * slot_queries : (g + 1) * slot_queries, :] = jnp.dot(
            probability, values_ref[:, columns], preferred_element_type=jnp.float32
        ) + own_weight * spread(value_ref[:, columns])

    z, y, s, _ = place()
    me = (z * 2 + y) * 2 + s
    block_rows = KEY_VALUE_HEADS * OWNER_ROW_SLOTS
    for j in range(GROUP_QUERIES):
        buffer[me, :, j * HEAD_SIZE : (j + 1) * HEAD_SIZE] = mixed[
            pl.ds(j, block_rows, stride=GROUP_QUERIES), :
        ].astype(jnp.bfloat16)
    enter()
    started = gather(buffer, send_sems, recv_sems, pieces)

    per = min(owners, 16)
    step = KEY_VALUE_HEADS if owners <= 16 else 1
    lane = lax.broadcasted_iota(jnp.int32, (rows, per * block_rows), 1)
    slot = (lane >> 5) * OWNER_ROW_SLOTS + (lane & 3)
    head = (lane >> 2) & 7

    def pick_block(block):
        everything = buffer[pl.ds(block * per, per)].reshape(per * block_rows, GROUP_WIDTH)
        wanted = destination_ref[...] - block * (per * OWNER_ROW_SLOTS)
        chosen = jnp.where(slot == wanted, head, -1)
        for first in range(0, KEY_VALUE_HEADS, step):
            pick = jnp.concatenate(
                [
                    jnp.where(chosen == first + g, 1.0, 0.0).astype(jnp.bfloat16)
                    for g in range(step)
                ],
                axis=0,
            )
            found = (
                jnp.dot(pick, everything, preferred_element_type=jnp.float32)
                .astype(jnp.bfloat16)
                .reshape(step, rows, GROUP_WIDTH)
            )
            if per == owners:
                picked[first : first + step] = found
            else:
                picked[first : first + step] += found

    if per == owners:
        pick_block(0)
    else:
        picked[...] = jnp.zeros_like(picked)
        pl.loop(0, owners // per)(pick_block)
    total[...] = jnp.zeros_like(total)

    @pl.loop(0, KEY_VALUE_HEADS)
    def _(g):
        weights(g).wait()
        part = pl.ds(pl.multiple_of(g * GROUP_WIDTH, GROUP_WIDTH), GROUP_WIDTH)
        total[...] += jnp.dot(picked[g], wo_ref[part, :], preferred_element_type=jnp.float32)

    out_ref[...] = total[...].astype(jnp.bfloat16)
    for wait in started:
        wait()


def attend(owners, rows, w_out, *operands):
    pieces = 2 if owners <= 16 else 1
    sends = (2 * owners - 3) * pieces
    block_rows = KEY_VALUE_HEADS * OWNER_ROW_SLOTS
    vmem, anywhere = pl.BlockSpec(memory_space=pltpu.VMEM), pl.BlockSpec(memory_space=pl.ANY)
    return pl.pallas_call(
        functools.partial(attend_kernel, owners, pieces),
        out_shape=jax.ShapeDtypeStruct((rows, w_out.shape[1]), jnp.bfloat16),
        in_specs=[anywhere] + [vmem] * len(operands),
        out_specs=vmem,
        scratch_shapes=[
            pltpu.VMEM(w_out.shape, jnp.bfloat16),
            pltpu.VMEM((block_rows * GROUP_QUERIES, HEAD_SIZE), jnp.float32),
            pltpu.VMEM((owners, block_rows, GROUP_WIDTH), jnp.bfloat16),
            pltpu.VMEM((KEY_VALUE_HEADS, rows, GROUP_WIDTH), jnp.bfloat16),
            pltpu.VMEM((rows, w_out.shape[1]), jnp.float32),
            pltpu.SemaphoreType.DMA((KEY_VALUE_HEADS,)),
            pltpu.SemaphoreType.DMA((sends,)),
            pltpu.SemaphoreType.DMA((owners, pieces)),
        ],
        compiler_params=pltpu.CompilerParams(
            collective_id=1, has_side_effects=True, vmem_limit_bytes=56 * 2**20
        ),
    )(w_out, *operands)


def per_device(
    hidden_in,
    norm_gain,
    w_query,
    key_projection,
    value_projection,
    w_out,
    paged_key_cache,
    paged_value_cache,
    key_scale,
    value_page_scale,
    row_owner,
    lengths,
    page_table,
):
    owners = lax.axis_size(("tensor", "side"))
    my_index = lax.axis_index(("tensor", "side"))
    row_count = hidden_in.shape[0]
    query_group_count = QUERY_HEADS // KEY_VALUE_HEADS
    owner_ids = row_owner[:, 0]
    row_numbers = jnp.arange(row_count)
    same_owner = owner_ids[:, None] == owner_ids[None, :]
    earlier = row_numbers[None, :] < row_numbers[:, None]
    slot_index = jnp.sum(jnp.where(same_owner & earlier, 1, 0), axis=1).astype(jnp.int32)
    destination = owner_ids * OWNER_ROW_SLOTS + slot_index
    received = project(
        owners, destination, hidden_in, norm_gain, w_query, key_projection, value_projection
    )
    heads = w_query.shape[1] // HEAD_SIZE
    key_columns = key_projection.shape[1]
    query_all = jnp.swapaxes(
        received[:, : heads * OWNER_ROW_SLOTS].reshape(QUERY_HEADS, OWNER_ROW_SLOTS, HEAD_SIZE),
        0,
        1,
    )
    pair = jnp.swapaxes(
        received[:, heads * OWNER_ROW_SLOTS : (heads + 1) * OWNER_ROW_SLOTS], 0, 1
    )
    every_key = pair[:, :, :key_columns].reshape(
        OWNER_ROW_SLOTS, KEY_VALUE_HEADS * HEAD_SIZE
    )
    every_value = pair[:, :, key_columns : 2 * key_columns].reshape(
        OWNER_ROW_SLOTS, KEY_VALUE_HEADS * HEAD_SIZE
    )
    mine = owner_ids == my_index
    slot_match = (jnp.arange(OWNER_ROW_SLOTS)[:, None] == slot_index[None, :]) & mine[None, :]
    slot_length = jnp.sum(jnp.where(slot_match, lengths[None, :], 0), axis=1)
    pages = page_table.shape[1]
    page_slot = jnp.arange(pages)
    holds = page_table[0][:, None] == jnp.arange(pages)[None, :]
    page_place = jnp.sum(jnp.where(holds, page_slot[:, None], 0), axis=0)
    token_in_row = (
        (page_place % SLOT_PAGES)[:, None] * PAGE_TOKENS + jnp.arange(PAGE_TOKENS)[None, :]
    ).reshape(1, pages * PAGE_TOKENS)
    token_slot = jnp.repeat(page_place // SLOT_PAGES, PAGE_TOKENS)[None, :]
    live = (
        (token_slot == jnp.arange(OWNER_ROW_SLOTS)[:, None])
        & (token_in_row < slot_length[:, None])
    ).astype(jnp.float32)
    key_factor = jnp.repeat(key_scale.T, PAGE_TOKENS, axis=1) * INV_ROOT
    value_factor = jnp.repeat(value_page_scale.T, PAGE_TOKENS, axis=1)
    token_position = slot_length.astype(jnp.float32)[:, None, None]
    turned_query = rotation_angles(
        query_all.astype(jnp.float32).reshape(OWNER_ROW_SLOTS, QUERY_HEADS, HEAD_SIZE),
        token_position,
    ).astype(jnp.bfloat16)
    turned_query = jnp.transpose(
        turned_query.reshape(
            OWNER_ROW_SLOTS, KEY_VALUE_HEADS, query_group_count, HEAD_SIZE
        ),
        (1, 0, 2, 3),
    ).reshape(KEY_VALUE_HEADS, OWNER_ROW_SLOTS * query_group_count, HEAD_SIZE)
    turned_key = (
        rotation_angles(
            every_key.astype(jnp.float32).reshape(OWNER_ROW_SLOTS, KEY_VALUE_HEADS, HEAD_SIZE),
            token_position,
        )
        .astype(jnp.bfloat16)
        .astype(jnp.float32)
        .reshape(OWNER_ROW_SLOTS, KEY_VALUE_HEADS * HEAD_SIZE)
    )
    return attend(
        owners,
        row_count,
        w_out,
        paged_key_cache.reshape(pages * PAGE_TOKENS, KEY_VALUE_HEADS * HEAD_SIZE),
        paged_value_cache.reshape(pages * PAGE_TOKENS, KEY_VALUE_HEADS * HEAD_SIZE),
        turned_query,
        turned_key,
        every_value.astype(jnp.float32),
        key_factor,
        value_factor,
        live,
        destination.astype(jnp.int32)[:, None],
    )


def solution(mesh):
    return jax.shard_map(
        per_device,
        mesh=mesh,
        in_specs=(
            P("groups", ("tensor", "side")),
            P(),
            P(None, ("tensor", "side")),
            P(None, ("tensor", "side")),
            P(None, ("tensor", "side")),
            P(None, ("tensor", "side")),
            P(("groups", "tensor", "side"), None, None),
            P(("groups", "tensor", "side"), None, None),
            P(("groups", "tensor", "side"), None),
            P(("groups", "tensor", "side"), None),
            P("groups", None),
            P("groups"),
            P(("groups", "tensor", "side"), None),
        ),
        out_specs=P("groups", ("tensor", "side")),
        check_vma=False,
    )
```
